256 devices in a mesh: range: 16 (over z, y_lo), blk: 16 (over y_hi, x, core).
Axes of the slice: x: 4, y: 4 (y_hi: 2, y_lo: 2; y = y_hi * 2 + y_lo), z: 8, core: 2. Of those that a mesh axis runs over, the one named last changes fastest.
Arguments:
- queries: bfloat16 [8192, 2048], P(('range', 'blk')), may hold values from -6 to 6
- routing: int32 [8192, 1], P(('range', 'blk')), may hold values from 0 to 15; in each aligned block of 32 rows (0 to 31, 32 to 63, ...) at most 8 rows name the same one
- windows: int32 [8192, 2], P(('range', 'blk')), may hold values from 0 to 2048, as said below
- shifts: int32 [8], replicated, may hold values from -256 to 256
- library: bfloat16 [32768, 2048], P(('range', 'blk')), may hold values from -6 to 6
Outputs:
- match: float32 [8192, 8], P(('range', 'blk'))
The draws below stay inside these ranges and needn't reach their ends.
Inputs may be any that keep to these rules, and one draw needn't show every extreme that they name: `windows`: lo < hi; hi - lo lies between 128 and 512, and equals 512 for some query. `routing`: within the queries of one device no range is named more than 8 times; some range is named exactly 8 times.
All inputs are finite; a program needn't handle non-finite values.
Results may differ from the reference program's by a relative error of at most 0.0003.
Values may be sent and summed in bfloat16 or wider, within the bound.
A program may use at most 256 MiB of HBM per device.

```python
import math
import jax
import jax.numpy as jnp
import numpy as np
from jax import lax

BINS = 2048
NOFF = 8
Q_DEV = 32
LIB_DEV = 128
CAP = 8
LIBR = 2048
QUERIES = 8192
LIBRARY = 32768
N_RANGE = 16


def draw_windows(key, part):
    key = jax.random.fold_in(key, 7)
    first, second = jax.random.split(key)
    spans = jax.random.randint(first, (QUERIES,), LIB_DEV, 4 * LIB_DEV + 1, dtype=jnp.int32)
    spans = jnp.where(jnp.arange(QUERIES) == 0, 4 * LIB_DEV, spans).astype(jnp.int32)
    lower = jax.random.randint(second, (QUERIES,), 0, LIBR - spans + 1, dtype=jnp.int32)
    return jnp.stack([lower, lower + spans], axis=1).astype(jnp.int32)


def plant(values, own_key, low, high):
    shape = values.shape
    spot = [jax.random.randint(jax.random.fold_in(own_key, axis), (), 0, shape[axis]) for axis in range(len(shape))]
    values = values.at[tuple(spot)].set(low)
    longest = shape.index(max(shape))
    spot[longest] = (spot[longest] + 1) % shape[longest]
    return values.at[tuple(spot)].set(high)


def block_scale(stream_key, dims, pieces, least, largest):
    def one(position, parts):
        steps = jax.random.uniform(jax.random.fold_in(jax.random.fold_in(stream_key, 6), position), (parts,), jnp.float32, least / len(pieces), largest / len(pieces))
        return jnp.repeat(jnp.exp(steps), dims[position] // parts).reshape((-1,) + (1,) * (len(dims) - position - 1))

    loudness = one(*pieces[0])
    for cut in pieces[1:]:
        loudness = loudness * one(*cut)
    return loudness


def deal_out(rng, own, number, rows, amount, top, bound, slope):
    sequence = jax.random.permutation(rng, amount)
    crowded, ordinary = portions_of(amount, rows * top, bound, slope, True), portions_of(amount, rows * top, bound, slope, False)
    places = jnp.arange(amount)

    def named(sizes, turn):
        used = int((sizes > 0).sum())
        fixed = max(1, used // 4)
        shifted = fixed + (places - fixed + turn * (used - fixed)) % max(1, amount - fixed)
        return jnp.zeros((amount,), jnp.int32).at[sequence[jnp.where(places < fixed, places, shifted)]].set(jnp.asarray(sizes, jnp.int32))

    sizes = jnp.where(number % 4 == 0, named(crowded, number // 4), named(ordinary, number - number // 4 - 1))
    mixed = jax.random.permutation(jax.random.fold_in(own, 3), amount)
    giver, sink = mixed[0:amount // 2 * 2:2], mixed[1:amount // 2 * 2:2]
    slack = jnp.minimum(sizes[giver] - 1, bound - sizes[sink]) // 2
    slack = jnp.where((giver == sequence[0]) | (sink == sequence[0]) | (sizes[sink] == 0), 0, jnp.maximum(slack, 0))
    shifted = jax.random.randint(jax.random.fold_in(own, 4), (amount // 2,), 0, 1 << 20) % (slack + 1)
    sizes = sizes.at[giver].add(-shifted).at[sink].add(shifted)
    labels = jnp.searchsorted(jnp.cumsum(sizes), jnp.arange(rows * top), side="right").astype(jnp.int32)
    listing = labels.reshape(top, rows).T
    listing = listing[jax.random.permutation(jax.random.fold_in(own, 1), rows)]
    turn = jax.random.randint(jax.random.fold_in(own, 2), (rows, 1), 0, top)
    return jnp.take_along_axis(listing, (jnp.arange(top)[None, :] + turn) % top, axis=1)


def portions_of(amount, total, limit, slope, full):
    loads = [(1 << 20) // math.isqrt(standing ** slope) + 1 for standing in range(1, amount + 1)]
    largest = limit if full else min(limit, max(-(-total // amount), total * loads[0] // sum(loads)))
    least = 1 if total - largest >= amount - 1 else 0
    holding, rest = [largest] + [least] * (amount - 1), total - largest - least * (amount - 1)
    while rest > 0:
        movable = [i for i in range(1, amount) if holding[i] < largest] or [i for i in range(1, amount) if holding[i] < limit]
        pool, left = sum([loads[i] for i in movable]), rest
        for i in movable:
            extra = min(limit - holding[i], max(1, left * loads[i] // pool), rest)
            holding[i] = holding[i] + extra
            rest = rest - extra
    return np.array(holding)


def noise(own_key, extent, scale, reach, shards=(), held_as=jnp.bfloat16):
    array = scale * jax.random.normal(own_key, extent, jnp.float32)
    if shards:
        array = array * block_scale(own_key, extent, shards, -0.22, 0.18)
    return jnp.clip(array, -reach, reach).astype(held_as)


def setup_inputs(seed: int = 0) -> dict:
    splits = jax.random.split(jax.random.key(seed), 6)
    queries = noise(splits[0], (QUERIES, BINS), 1.0, 6.0, ((0, 256),))
    routing_keys = jax.random.split(jax.random.fold_in(splits[1], 1), QUERIES // Q_DEV)
    routing_turns = jax.random.permutation(jax.random.fold_in(splits[1], 3), QUERIES // Q_DEV)
    routing = jax.vmap(lambda own, number: deal_out(jax.random.fold_in(splits[1], 2), own, number, Q_DEV, N_RANGE, 1, CAP, 2))(routing_keys, routing_turns).reshape((QUERIES, 1))
    windows = draw_windows(jax.random.fold_in(splits[5], 71), 0)
    shifts = plant(jax.random.randint(splits[3], (NOFF,), 0 - BINS // 8, BINS // 8 + 1), jax.random.fold_in(splits[3], 1), 0 - BINS // 8, (BINS // 8 + 1) - 1).astype(jnp.int32)
    library = noise(splits[4], (LIBRARY, BINS), 1.0, 6.0, ((0, 256),))
    return {"queries": queries, "routing": routing, "windows": windows, "shifts": shifts, "library": library}


def shift_bins(spectra, shift):
    width = spectra.shape[-1]
    rolled = jnp.roll(spectra, shift, axis=-1)
    source = jnp.arange(width, dtype=jnp.int32) - shift
    keep = (source >= 0) & (source < width)
    return jnp.where(keep[None, :], rolled, jnp.zeros_like(rolled))


def reference(queries, routing, windows, shifts, library):
    widest = 4 * LIB_DEV
    scale = jnp.float32(BINS) ** -0.5
    group = Q_DEV
    blocks = queries.reshape(QUERIES // group, group, BINS)
    dest = routing[:, 0].reshape(QUERIES // group, group)
    lower = windows[:, 0].reshape(QUERIES // group, group)
    upper = windows[:, 1].reshape(QUERIES // group, group)

    def one_block(items):
        spectra, target, start, stop = items
        index = start[:, None] + jnp.arange(widest, dtype=jnp.int32)[None, :]
        valid = index < stop[:, None]
        rows = target[:, None] * LIBR + jnp.minimum(index, LIBR - 1)
        chosen = library[rows.reshape(-1)].reshape(group, widest, BINS)
        moved = jnp.stack([shift_bins(spectra, shifts[o]) for o in range(NOFF)], 0)
        scores = jnp.einsum("obk,bwk->obw", moved.astype(jnp.float32), chosen.astype(jnp.float32),
                            precision=lax.Precision.HIGHEST)
        level = jnp.maximum(scores * scale, 0.0)
        total = jnp.sum(jnp.where(valid[None], level * level, 0.0), axis=2)
        return (total / (stop - start).astype(jnp.float32)[None, :]).T

    result = lax.map(one_block, (blocks, dest, lower, upper))
    return result.reshape(QUERIES, NOFF)
```

```python
import functools

import jax
import jax.numpy as jnp
from jax import lax
from jax.experimental import pallas as pl
from jax.experimental.pallas import tpu as pltpu
from jax.sharding import PartitionSpec as P

MESH = pl.DeviceIdType.MESH
LANES = 128
PAD = 256


def column_to_row(column, width, period):
    rows = column.shape[0]
    p = lax.broadcasted_iota(jnp.int32, (rows, width), 0)
    c = lax.broadcasted_iota(jnp.int32, (rows, width), 1)
    same = p == lax.rem(c, period)
    return jnp.sum(jnp.where(same, column, 0.0), axis=0, keepdims=True)


def kernel(
    n_range, n_x, sizes,
    q_ref, routing_ref, windows_ref, shifts_ref, lib_ref, out_ref,
    tx, rx, groups, passing, lt, padded, shifted, weight, res, part, total, ret,
    lib_send, lib_recv, a2a_send, a2a_recv, sib_send, sib_recv, y_send, y_recv,
    part_send, part_recv, ret_send, ret_recv,
):
    q_count, width, cap, lib_dev, n_off = sizes
    half = width // 2
    slots = n_range * cap
    me = lax.axis_index("range")
    blk = lax.axis_index("blk")
    core = lax.rem(blk, 2)
    x = lax.rem(lax.div(blk, 2), n_x)
    yh = lax.div(blk, 2 * n_x)
    z = lax.div(me, 2)
    yl = lax.rem(me, 2)

    def block_of(yh_, x_, core_):
        return yh_ * (2 * n_x) + x_ * 2 + core_

    right = {"blk": block_of(yh, lax.rem(x + 1, n_x), core)}
    left = {"blk": block_of(yh, lax.rem(x + n_x - 1, n_x), core)}
    sibling = {"blk": block_of(yh, x, 1 - core)}
    across = {"blk": block_of(1 - yh, x, core)}
    diagonal = {"blk": block_of(1 - yh, x, 1 - core)}
    y = yh * 2 + yl

    def along_y(step):
        there = lax.rem(y + step, 4)
        return {
            "range": z * 2 + lax.rem(there, 2),
            "blk": block_of(lax.div(there, 2), x, core),
        }

    onward = along_y(1 + 2 * core)
    backward = along_y(3 - 2 * core)

    barrier = pltpu.get_barrier_semaphore()

    def greet(k, carry):
        pl.semaphore_signal(
            barrier, inc=1, device_id={"range": lax.rem(me + k, n_range)}, device_id_type=MESH
        )
        return carry

    lax.fori_loop(1, n_range, greet, 0)
    near = (right, left, sibling, across, diagonal, onward, backward)
    for device in near:
        pl.semaphore_signal(barrier, inc=1, device_id=device, device_id_type=MESH)

    target = routing_ref[...].astype(jnp.float32)
    t_row = column_to_row(target, 2 * q_count, q_count)
    p = lax.broadcasted_iota(jnp.int32, (q_count, 2 * q_count), 0)
    c = lax.broadcasted_iota(jnp.int32, (q_count, 2 * q_count), 1)
    earlier = (target == t_row) & (p < lax.rem(c, q_count))
    slot_row = t_row * cap + jnp.sum(jnp.where(earlier, 1.0, 0.0), axis=0, keepdims=True)
    r = lax.broadcasted_iota(jnp.int32, (2 * slots, 2 * q_count), 0)
    c = lax.broadcasted_iota(jnp.int32, (2 * slots, 2 * q_count), 1)
    r_slot = lax.div(r, 2 * cap) * cap + lax.rem(r, cap)
    r_half = lax.rem(lax.div(r, cap), 2)
    hit = (r_slot.astype(jnp.float32) == slot_row) & (r_half == lax.div(c, q_count))
    table = jnp.where(hit, 1.0, 0.0).astype(jnp.bfloat16)
    stacked = jnp.concatenate([q_ref[:, :half], q_ref[:, half:]], axis=0)
    tx[:, :, :half] = (
        jnp.dot(table, stacked, preferred_element_type=jnp.float32)
        .astype(jnp.bfloat16)
        .reshape(n_range, 2 * cap, half)
    )
    first = windows_ref[:, 0:1]
    last = windows_ref[:, 1:2]
    lane = lax.broadcasted_iota(jnp.int32, (q_count, LANES), 1)
    coded = jnp.where(
        lane == 0, lax.div(first, 64),
        jnp.where(lane == 1, lax.rem(first, 64),
                  jnp.where(lane == 2, lax.div(last, 64),
                            jnp.where(lane == 3, lax.rem(last, 64), 0))))
    coded = coded.astype(jnp.float32).astype(jnp.bfloat16)
    coded = jnp.concatenate([coded, coded], axis=0)
    tx[:, :, half:] = (
        jnp.dot(table, coded, preferred_element_type=jnp.float32)
        .astype(jnp.bfloat16)
        .reshape(n_range, 2 * cap, LANES)
    )
    rx[me] = tx[me]

    pieces = lt.shape[1]
    depth = width // pieces
    for k in range(pieces):
        block = lib_ref[:, k * depth:(k + 1) * depth].astype(jnp.float32).T
        padded[0, PAD + k * depth:PAD + (k + 1) * depth, :] = block
        lt[0, k] = block.astype(jnp.bfloat16)
    for b in range(n_x):
        padded[b, :PAD, :] = jnp.zeros((PAD, LANES), jnp.float32)
        padded[b, PAD + width:, :] = jnp.zeros((PAD, LANES), jnp.float32)

    pl.semaphore_wait(barrier, n_range - 1 + len(near))

    def a2a(k):
        there = lax.rem(me + k, n_range)
        return pltpu.make_async_remote_copy(
            src_ref=tx.at[there], dst_ref=rx.at[me],
            send_sem=a2a_send.at[there], recv_sem=a2a_recv.at[me],
            device_id={"range": there}, device_id_type=MESH,
        )

    def a2a_from(source):
        return pltpu.make_async_remote_copy(
            src_ref=tx.at[source], dst_ref=rx.at[source],
            send_sem=a2a_send.at[source], recv_sem=a2a_recv.at[source],
            device_id={"range": source}, device_id_type=MESH,
        )

    def lib_copy(way, k, source, landing, device):
        return pltpu.make_async_remote_copy(
            src_ref=lt.at[source, k], dst_ref=lt.at[landing, k],
            send_sem=lib_send.at[way, k], recv_sem=lib_recv.at[way, k],
            device_id=device, device_id_type=MESH,
        )

    def start_a2a(k, carry):
        a2a(k).start()
        return carry

    split = pieces // 2
    order = list(range(pieces))
    to_right = {k: lib_copy(0, k, 0, 1, right) for k in order}
    to_left = {k: lib_copy(1, k, 0, 2, left) for k in order}
    on_right = {k: lib_copy(2, k, 1, 3, right) for k in order[:split]}
    on_left = {k: lib_copy(2, k, 2, 3, left) for k in order[split:]}

    for k in order[:split]:
        to_right[k].start()
        to_left[k + split].start()
    lax.fori_loop(1, n_range, start_a2a, 0)
    for k in order[:split]:
        to_right[k + split].start()
        to_left[k].start()

    rows = 256

    def shift_block(b):
        def one(step, carry):
            o = lax.div(step, width // rows)
            at = pl.multiple_of(lax.rem(step, width // rows) * rows, rows)
            moved = padded[b, pl.ds(PAD + shifts_ref[o] + at, rows), :]
            shifted[o, pl.ds(at, rows), b * LANES:(b + 1) * LANES] = moved.astype(jnp.bfloat16)
            return carry

        lax.fori_loop(0, n_off * (width // rows), one, 0)

    def widen(b):
        for k in order:
            padded[b, PAD + k * depth:PAD + (k + 1) * depth, :] = lt[b, k].astype(jnp.float32)

    shift_block(0)

    for k in range(split):
        to_right[k].wait_recv()
        on_right[k].start()
        to_left[k + split].wait_recv()
        on_left[k + split].start()

    subs = groups.shape[1]
    sub_rows = groups.shape[2]
    per_sub = n_range // subs
    pr = lax.broadcasted_iota(jnp.int32, (sub_rows, 2 * sub_rows), 0)
    pc = lax.broadcasted_iota(jnp.int32, (sub_rows, 2 * sub_rows), 1)
    source_row = lax.div(pr, cap) * (2 * cap) + lax.rem(pr, cap)
    pick_low = jnp.where(pc == source_row, 1.0, 0.0).astype(jnp.bfloat16)
    pick_high = jnp.where(pc == source_row + cap, 1.0, 0.0).astype(jnp.bfloat16)

    def sib_copy(way, j, group, landing):
        return pltpu.make_async_remote_copy(
            src_ref=groups.at[group, j], dst_ref=groups.at[landing, j],
            send_sem=sib_send.at[way, j], recv_sem=sib_recv.at[way, j],
            device_id=sibling, device_id_type=MESH,
        )

    def y_first(j):
        return pltpu.make_async_remote_copy(
            src_ref=groups.at[0, j], dst_ref=passing.at[j],
            send_sem=y_send.at[0, j], recv_sem=y_recv.at[0, j],
            device_id=onward, device_id_type=MESH,
        )

    def y_second(j):
        return pltpu.make_async_remote_copy(
            src_ref=passing.at[j], dst_ref=groups.at[2, j],
            send_sem=y_send.at[1, j], recv_sem=y_recv.at[1, j],
            device_id=onward, device_id_type=MESH,
        )

    home = lax.div(me, per_sub)

    def sub_of(k):
        return lax.rem(home + k, subs)

    def gather_sub(k, carry):
        j = sub_of(k)

        def arrive(i, inner):
            source = j * per_sub + i

            @pl.when(source != me)
            def _():
                a2a_from(source).wait_recv()

            return inner

        lax.fori_loop(0, per_sub, arrive, 0)
        piece = rx[pl.ds(j * per_sub, per_sub)].reshape(2 * sub_rows, half + LANES)
        groups[0, j, :, :half] = jnp.dot(
            pick_low, piece[:, :half], preferred_element_type=jnp.float32
        ).astype(jnp.bfloat16)
        groups[0, j, :, half:width] = jnp.dot(
            pick_high, piece[:, :half], preferred_element_type=jnp.float32
        ).astype(jnp.bfloat16)
        groups[0, j, :, width:] = jnp.dot(
            pick_low, piece[:, half:], preferred_element_type=jnp.float32
        ).astype(jnp.bfloat16)
        y_first(j).start()
        sib_copy(0, j, 0, 1).start()
        return carry

    lax.fori_loop(0, subs, gather_sub, 0)

    def pass_on(k, carry):
        j = sub_of(k)
        y_first(j).wait_recv()
        y_second(j).start()
        return carry

    lax.fori_loop(0, subs, pass_on, 0)

    for k in range(split):
        to_right[k + split].wait_recv()
        to_left[k].wait_recv()
    widen(1)
    shift_block(1)
    widen(2)
    shift_block(2)
    for k in range(split):
        on_right[k].wait_recv()
        on_left[k + split].wait_recv()
    widen(3)
    shift_block(3)

    wide = n_x * LANES
    col = lax.broadcasted_iota(jnp.int32, (1, wide), 1)
    nth = lax.div(col, LANES)
    away = jnp.where(nth == 0, 0, jnp.where(nth == 1, n_x - 1, jnp.where(nth == 2, 1, 2)))
    block_at = block_of(yh, lax.rem(x + away, n_x), core)
    index = (block_at * LANES + lax.rem(col, LANES)).astype(jnp.float32)
    m = 2 * slots

    def score_pair(pair):
        bounds = groups[2 * pair:2 * pair + 2, :, :, width:].reshape(m, LANES).astype(jnp.float32)
        lane = lax.broadcasted_iota(jnp.int32, (m, LANES), 1)
        low = jnp.sum(
            jnp.where(lane == 0, bounds * 64.0, jnp.where(lane == 1, bounds, 0.0)), axis=1, keepdims=True
        )
        high = jnp.sum(
            jnp.where(lane == 2, bounds * 64.0, jnp.where(lane == 3, bounds, 0.0)), axis=1, keepdims=True
        )
        weight[...] = jnp.where((index >= low) & (index < high), 1.0, 0.0)
        res[2 * pair:2 * pair + 2] = jnp.zeros((2, slots, LANES), jnp.float32)

        def one(o, carry):
            spectra = groups[2 * pair:2 * pair + 2, :, :, :width].reshape(m, width)
            scores = jnp.dot(spectra, shifted[o], preferred_element_type=jnp.float32)
            level = jnp.maximum(scores, 0.0)
            kept = level * level * weight[...]
            summed = jnp.sum(kept, axis=1, keepdims=True)
            here = lax.broadcasted_iota(jnp.int32, (m, LANES), 1) == o
            old = res[2 * pair:2 * pair + 2].reshape(m, LANES)
            res[2 * pair:2 * pair + 2] = jnp.where(here, summed, old).reshape(2, slots, LANES)
            return carry

        lax.fori_loop(0, n_off, one, 0)

    def part_copy(g, device):
        return pltpu.make_async_remote_copy(
            src_ref=res.at[g], dst_ref=part.at[g - 1],
            send_sem=part_send.at[g - 1], recv_sem=part_recv.at[g - 1],
            device_id=device, device_id_type=MESH,
        )

    parts = [part_copy(1, sibling), part_copy(2, across), part_copy(3, diagonal)]

    def all_subs(body):
        def one(k, carry):
            body(sub_of(k))
            return carry

        lax.fori_loop(0, subs, one, 0)

    all_subs(lambda j: sib_copy(0, j, 0, 1).wait_recv())
    score_pair(0)
    parts[0].start()

    def relay(j):
        y_second(j).wait_recv()
        sib_copy(1, j, 2, 3).start()

    all_subs(relay)
    all_subs(lambda j: sib_copy(1, j, 2, 3).wait_recv())
    score_pair(1)
    parts[1].start()
    parts[2].start()
    for one_part in parts:
        one_part.wait_recv()
    total[...] = (res[0] + part[0] + part[1] + part[2]).reshape(n_range, cap, LANES)

    def back(k):
        there = lax.rem(me + k, n_range)
        return pltpu.make_async_remote_copy(
            src_ref=total.at[there], dst_ref=ret.at[me],
            send_sem=ret_send.at[there], recv_sem=ret_recv.at[me],
            device_id={"range": there}, device_id_type=MESH,
        )

    def back_from(source):
        return pltpu.make_async_remote_copy(
            src_ref=total.at[source], dst_ref=ret.at[source],
            send_sem=ret_send.at[source], recv_sem=ret_recv.at[source],
            device_id={"range": source}, device_id_type=MESH,
        )

    def start_back(k, carry):
        back(k).start()
        return carry

    lax.fori_loop(1, n_range, start_back, 0)
    ret[me] = total[me]

    def finish_sends(k, carry):
        a2a(k).wait_send()
        return carry

    lax.fori_loop(1, n_range, finish_sends, 0)
    for copies in (to_right, to_left, on_right, on_left):
        for k in copies:
            copies[k].wait_send()

    def finish_groups(j):
        y_first(j).wait_send()
        y_second(j).wait_send()
        sib_copy(0, j, 0, 1).wait_send()
        sib_copy(1, j, 2, 3).wait_send()

    all_subs(finish_groups)
    for one_part in parts:
        one_part.wait_send()

    def finish_back(k, carry):
        back_from(lax.rem(me + k, n_range)).wait_recv()
        return carry

    lax.fori_loop(1, n_range, finish_back, 0)

    t_wide = column_to_row(target, q_count, q_count)
    p = lax.broadcasted_iota(jnp.int32, (q_count, q_count), 0)
    c = lax.broadcasted_iota(jnp.int32, (q_count, q_count), 1)
    place = jnp.sum(jnp.where((target == t_wide) & (c < p), 1.0, 0.0), axis=1, keepdims=True)
    slot_column = target * cap + place
    spot = lax.broadcasted_iota(jnp.int32, (q_count, slots), 1).astype(jnp.float32)
    choose = jnp.where(spot == slot_column, 1.0, 0.0)
    answer = jnp.dot(
        choose, ret[...].reshape(slots, LANES),
        precision=lax.Precision.HIGHEST, preferred_element_type=jnp.float32,
    )
    span = (windows_ref[:, 1:2] - windows_ref[:, 0:1]).astype(jnp.float32) * float(width)
    out_ref[...] = (answer / span)[:, :n_off]

    def finish_returns(k, carry):
        back(k).wait_send()
        return carry

    lax.fori_loop(1, n_range, finish_returns, 0)


def local(queries, routing, windows, shifts, library):
    n_range = lax.axis_size("range")
    n_x = lax.axis_size("blk") // 4
    q_count, width = queries.shape
    lib_dev = library.shape[0]
    n_off = shifts.shape[0]
    cap = q_count // 4
    slots = n_range * cap
    subs = 4
    pieces = 4
    bf16, f32 = jnp.bfloat16, jnp.float32
    dma = pltpu.SemaphoreType.DMA
    vmem = pl.BlockSpec(memory_space=pltpu.VMEM)
    return pl.pallas_call(
        functools.partial(kernel, n_range, n_x, (q_count, width, cap, lib_dev, n_off)),
        out_shape=jax.ShapeDtypeStruct((q_count, n_off), f32),
        in_specs=[vmem, vmem, vmem, pl.BlockSpec(memory_space=pltpu.SMEM), vmem],
        out_specs=vmem,
        scratch_shapes=[
            pltpu.VMEM((n_range, 2 * cap, width // 2 + LANES), bf16),
            pltpu.VMEM((n_range, 2 * cap, width // 2 + LANES), bf16),
            pltpu.VMEM((4, subs, slots // subs, width + LANES), bf16),
            pltpu.VMEM((subs, slots // subs, width + LANES), bf16),
            pltpu.VMEM((n_x, pieces, width // pieces, lib_dev), bf16),
            pltpu.VMEM((n_x, width + 2 * PAD, lib_dev), f32),
            pltpu.VMEM((n_off, width, n_x * lib_dev), bf16),
            pltpu.VMEM((2 * slots, n_x * lib_dev), f32),
            pltpu.VMEM((4, slots, LANES), f32),
            pltpu.VMEM((3, slots, LANES), f32),
            pltpu.VMEM((n_range, cap, LANES), f32),
            pltpu.VMEM((n_range, cap, LANES), f32),
            dma((3, pieces)), dma((3, pieces)),
            dma((n_range,)), dma((n_range,)),
            dma((2, subs)), dma((2, subs)),
            dma((2, subs)), dma((2, subs)),
            dma((3,)), dma((3,)),
            dma((n_range,)), dma((n_range,)),
        ],
        compiler_params=pltpu.CompilerParams(
            collective_id=0, has_side_effects=True, vmem_limit_bytes=56 * 1024 * 1024
        ),
    )(queries, routing, windows, shifts, library)


def solution(mesh):
    both = ("range", "blk")
    in_specs = (P(both, None), P(both, None), P(both, None), P(), P(both, None))
    return jax.shard_map(
        local, mesh=mesh, in_specs=in_specs, out_specs=P(both, None), check_vma=False
    )
```

```python
import functools

import jax
import jax.numpy as jnp
from jax import lax
from jax.experimental import pallas as pl
from jax.experimental.pallas import tpu as pltpu
from jax.sharding import PartitionSpec as P

MESH = pl.DeviceIdType.MESH
LANES = 128
PAD = 256
INVERSE = (0, 2, 1, 3)


def kernel(
    n_z, n_x, sizes,
    q_ref, routing_ref, windows_ref, shifts_ref, lib_ref, out_ref,
    tx, rx, groups, other, lt, padded, shifted, weight, acc, res, part_out, part, total, ret,
    z_send, z_recv, y_send, y_recv, sib_send, sib_recv, lib_send, lib_recv,
    part_send, part_recv, ret_send, ret_recv,
):
    q_count, width, cap, n_off = sizes
    n_pos = n_z // 2
    slots = 2 * n_z * cap
    pair = 2 * cap
    f32, bf16 = jnp.float32, jnp.bfloat16
    me = lax.axis_index("range")
    blk = lax.axis_index("blk")
    core = lax.rem(blk, 2)
    x = lax.rem(lax.div(blk, 2), n_x)
    yh = lax.div(blk, 2 * n_x)
    z = lax.div(me, 2)
    yl = lax.rem(me, 2)
    y = yh * 2 + yl

    def device(dz, dy, dx, dc):
        y_there = lax.rem(y + dy, 4)
        x_there = lax.rem(x + dx, n_x)
        return {
            "range": lax.rem(z + dz, n_z) * 2 + lax.rem(y_there, 2),
            "blk": lax.div(y_there, 2) * (2 * n_x) + x_there * 2 + lax.rem(core + dc, 2),
        }

    def remote(src, dst, send, recv, there):
        return pltpu.make_async_remote_copy(
            src_ref=src, dst_ref=dst, send_sem=send, recv_sem=recv,
            device_id=there, device_id_type=MESH,
        )

    y_step = (0, 1, 3, 2)
    barrier = pltpu.get_barrier_semaphore()
    greeted = [device(dz, 0, 0, 0) for dz in range(1, n_z)]
    greeted += [device(0, y_step[k], 0, dc) for k in range(4) for dc in range(2) if k or dc]
    greeted += [device(0, 0, dx, 0) for dx in range(1, n_x)]
    for there in greeted:
        pl.semaphore_signal(barrier, inc=1, device_id=there, device_id_type=MESH)

    t_row = routing_ref[...].astype(f32)
    p = lax.broadcasted_iota(jnp.int32, (q_count, q_count), 0)
    c = lax.broadcasted_iota(jnp.int32, (q_count, q_count), 1)
    t_column = jnp.sum(jnp.where(p == c, t_row, 0.0), axis=1, keepdims=True)
    earlier = (t_column == t_row) & (p < c)
    place = jnp.sum(jnp.where(earlier, 1.0, 0.0), axis=0, keepdims=True)
    slot_row = t_row * cap + place
    r = lax.broadcasted_iota(jnp.int32, (slots, q_count), 0).astype(f32)
    table = jnp.where(r == slot_row, 1.0, 0.0).astype(bf16)
    tx[:, :, :width] = (
        jnp.dot(table, q_ref[...], preferred_element_type=f32).astype(bf16).reshape(n_z, pair, width)
    )
    first = windows_ref[0:1, :]
    last = windows_ref[1:2, :]
    line = lax.broadcasted_iota(jnp.int32, (LANES, q_count), 0)
    coded = jnp.where(
        line == 0, lax.div(first, 64),
        jnp.where(line == 1, lax.rem(first, 64),
                  jnp.where(line == 2, lax.div(last, 64),
                            jnp.where(line == 3, lax.rem(last, 64), 0))))
    coded = coded.astype(f32).astype(bf16)
    tx[:, :, width:] = (
        lax.dot_general(table, coded, (((1,), (1,)), ((), ())), preferred_element_type=f32)
        .astype(bf16).reshape(n_z, pair, LANES)
    )
    rx[z] = tx[z]

    pieces = lt.shape[1]
    depth = width // pieces
    for k in range(pieces):
        block = lib_ref[:, k * depth:(k + 1) * depth].astype(f32).T
        padded[0, PAD + k * depth:PAD + (k + 1) * depth, :] = block
        lt[0, k] = block.astype(bf16)
    for b in range(n_x):
        padded[b, :PAD, :] = jnp.zeros((PAD, LANES), f32)
        padded[b, PAD + width:, :] = jnp.zeros((PAD, LANES), f32)

    pl.semaphore_wait(barrier, len(greeted))

    def z_copy(dz):
        there = lax.rem(z + dz, n_z)
        return remote(tx.at[there], rx.at[z], z_send.at[there], z_recv.at[z], device(dz, 0, 0, 0))

    def z_from(source):
        return remote(
            tx.at[source], rx.at[source], z_send.at[source], z_recv.at[source],
            device(lax.rem(source - z + n_z, n_z), 0, 0, 0),
        )

    def lib_copy(dx, k):
        landing = n_x - dx
        return remote(
            lt.at[0, k], lt.at[landing, k], lib_send.at[dx - 1, k], lib_recv.at[landing - 1, k],
            device(0, 0, dx, 0),
        )

    def lib_from(b, k):
        return remote(
            lt.at[0, k], lt.at[b, k], lib_send.at[b - 1, k], lib_recv.at[b - 1, k],
            device(0, 0, b, 0),
        )

    z_order = [1, n_z - 1, 2, n_z - 2, 3, n_z - 3, 4]
    for dz in z_order:
        z_copy(dz).start()
    for dx in (1, n_x - 1, 2):
        for k in range(pieces):
            lib_copy(dx, k).start()

    rows = 256

    def shift_block(b):
        def one(step, carry):
            o = lax.div(step, width // rows)
            at = pl.multiple_of(lax.rem(step, width // rows) * rows, rows)
            lane = pl.multiple_of(o * LANES, LANES)
            moved = padded[b, pl.ds(PAD + shifts_ref[o] + at, rows), :]
            shifted[b, pl.ds(at, rows), pl.ds(lane, LANES)] = moved.astype(bf16)
            return carry

        lax.fori_loop(0, n_off * (width // rows), one, 0)

    def take_block(b):
        for k in range(pieces):
            lib_from(b, k).wait_recv()
            padded[b, PAD + k * depth:PAD + (k + 1) * depth, :] = lt[b, k].astype(f32)
        shift_block(b)

    pr = lax.broadcasted_iota(jnp.int32, (2 * pair, 2 * pair), 0)
    pc = lax.broadcasted_iota(jnp.int32, (2 * pair, 2 * pair), 1)
    upper = lax.div(pr, pair)
    source_half = jnp.where(upper == 0, yl, 1 - yl)
    within = lax.rem(pr, pair)
    from_row = lax.div(within, cap) * pair + source_half * cap + lax.rem(within, cap)
    pick = jnp.where(pc == from_row, 1.0, 0.0).astype(bf16)
    home = lax.div(z, 2)
    hop = (0, n_pos - 1, 1, 2)

    def y_copy(k, pos):
        src = groups.at[pos, 0, 0] if k == 3 else other.at[pos]
        landing = INVERSE[k]
        return remote(
            src, groups.at[pos, 0, landing], y_send.at[k - 1, pos], y_recv.at[landing - 1, pos],
            device(0, y_step[k], 0, 0),
        )

    def y_from(k, pos):
        return remote(
            other.at[pos], groups.at[pos, 0, k], y_send.at[k - 1, pos], y_recv.at[k - 1, pos],
            device(0, y_step[k], 0, 0),
        )

    def sib_copy(k, pos):
        return remote(
            groups.at[pos, 0, k], groups.at[pos, 1, k], sib_send.at[k, pos], sib_recv.at[k, pos],
            device(0, 0, 0, 1),
        )

    def send_pos(pos):
        u = lax.rem(home + hop[pos], n_pos)
        for i in range(2):
            source = u * 2 + i

            @pl.when(source != z)
            def _():
                z_from(source).wait_recv()

        piece = rx[pl.ds(u * 2, 2)].reshape(2 * pair, width + LANES)
        parted = jnp.dot(pick, piece, preferred_element_type=f32).astype(bf16)
        groups[pos, 0, 0] = parted[:pair]
        other[pos] = parted[pair:]
        for k in (3, 1, 2):
            y_copy(k, pos).start()
        sib_copy(0, pos).start()

    def relay(pos):
        for k in (1, 2, 3):
            y_from(k, pos).wait_recv()
            sib_copy(k, pos).start()

    def settle(pos):
        for k in range(4):
            sib_copy(k, pos).wait_recv()

    wide = n_x * LANES
    col = lax.broadcasted_iota(jnp.int32, (1, wide), 1)
    block_at = yh * (2 * n_x) + lax.rem(x + lax.div(col, LANES), n_x) * 2 + core
    index = (block_at * LANES + lax.rem(col, LANES)).astype(f32)
    m = 8 * pair * 2

    def weigh(h):
        bounds = groups[2 * h:2 * h + 2, :, :, :, width:].reshape(m, LANES).astype(f32)
        lane = lax.broadcasted_iota(jnp.int32, (m, LANES), 1)
        low = jnp.sum(
            jnp.where(lane == 0, bounds * 64.0, jnp.where(lane == 1, bounds, 0.0)), axis=1, keepdims=True
        )
        high = jnp.sum(
            jnp.where(lane == 2, bounds * 64.0, jnp.where(lane == 3, bounds, 0.0)), axis=1, keepdims=True
        )
        weight[h] = jnp.where((index >= low) & (index < high), 1.0, 0.0)

    def score(h, b, fresh):
        spectra = groups[2 * h:2 * h + 2, :, :, :, :width].reshape(m, width)
        for part_of in range(2):
            at = part_of * 4 * LANES
            scores = jnp.dot(spectra, shifted[b, :, at:at + 4 * LANES], preferred_element_type=f32)
            for i in range(4):
                level = jnp.maximum(scores[:, i * LANES:(i + 1) * LANES], 0.0)
                kept = level * level * weight[h, :, b * LANES:(b + 1) * LANES]
                o = part_of * 4 + i
                acc[h, o] = kept if fresh else acc[h, o] + kept

    def gather_scores(h):
        lane = lax.broadcasted_iota(jnp.int32, (m, LANES), 1)
        value = jnp.zeros((m, LANES), f32)
        for o in range(n_off):
            value = jnp.where(lane == o, jnp.sum(acc[h, o], axis=1, keepdims=True), value)
        res[2 * h:2 * h + 2] = value.reshape(2, 2, 4, pair, LANES)

    shift_block(0)
    for pos in range(n_pos):
        send_pos(pos)
        if pos:
            relay(pos - 1)
    relay(n_pos - 1)
    for pos in range(n_pos):
        settle(pos)
    weigh(0)
    weigh(1)
    score(0, 0, True)
    score(1, 0, True)
    for b in (1, 3, 2):
        take_block(b)
        score(0, b, False)
        score(1, b, False)
    gather_scores(0)
    gather_scores(1)

    def part_copy(k, dc):
        return remote(
            part_out.at[2 * k + dc], part.at[2 * INVERSE[k] + dc],
            part_send.at[2 * k + dc], part_recv.at[2 * INVERSE[k] + dc],
            device(0, y_step[k], 0, dc),
        )

    def part_from(k, dc):
        return remote(
            part_out.at[2 * k + dc], part.at[2 * k + dc],
            part_send.at[2 * k + dc], part_recv.at[2 * k + dc],
            device(0, y_step[k], 0, dc),
        )

    lane = lax.broadcasted_iota(jnp.int32, (n_off, LANES), 1)
    mine = lax.div(lane, LANES // 2) == yl
    partners = [(k, dc) for k in (3, 1, 2, 0) for dc in range(2) if k or dc]
    for k, dc in partners + [(0, 0)]:
        column = res[:, dc, k].reshape(n_pos * pair, LANES)
        tile = jnp.concatenate([column, column], axis=0).T[:n_off]
        part_out[2 * k + dc] = jnp.where(mine, tile, 0.0)
        if k or dc:
            part_copy(k, dc).start()
    summed = part_out[0]
    for k, dc in partners:
        part_from(k, dc).wait_recv()
        summed = summed + part[2 * k + dc]
    total[...] = summed

    def ret_copy(dz):
        there = lax.rem(z + dz, n_z)
        return remote(total, ret.at[z], ret_send.at[there], ret_recv.at[z], device(dz, 0, 0, 0))

    def ret_from(dz):
        source = lax.rem(z + dz, n_z)
        return remote(
            total, ret.at[source], ret_send.at[source], ret_recv.at[source], device(dz, 0, 0, 0)
        )

    for dz in [4] + z_order[:-1][::-1]:
        ret_copy(dz).start()
    ret[z] = summed

    for dz in z_order:
        z_copy(dz).wait_send()
    for dx in range(1, n_x):
        for k in range(pieces):
            lib_copy(dx, k).wait_send()
    for pos in range(n_pos):
        for k in (1, 2, 3):
            y_copy(k, pos).wait_send()
        for k in range(4):
            sib_copy(k, pos).wait_send()
    for k, dc in partners:
        part_copy(k, dc).wait_send()

    half_row = jnp.floor(t_row * 0.5)
    z_there = half_row
    yl_there = t_row - 2.0 * half_row
    delta = home.astype(f32) - jnp.floor(z_there * 0.5)
    delta = jnp.where(delta < 0.0, delta + n_pos, delta)
    pos_there = jnp.where(delta == 0.0, 0.0, jnp.where(delta == n_pos - 1.0, 1.0, delta + 1.0))
    spot = (
        z_there * LANES + yl_there * (LANES // 2) + pos_there * pair
        + lax.rem(z, 2).astype(f32) * cap + place
    )
    line = lax.broadcasted_iota(jnp.int32, (n_z * LANES, q_count), 0).astype(f32)
    choose = jnp.where(line == spot, 1.0, 0.0)

    for dz in z_order:
        ret_from(dz).wait_recv()
    every = jnp.concatenate([ret[i] for i in range(n_z)], axis=1)
    answer = jnp.dot(every, choose, precision=lax.Precision.HIGHEST, preferred_element_type=f32)
    span = (last - first).astype(f32) * float(width)
    out_ref[...] = answer / span

    for dz in z_order:
        ret_copy(dz).wait_send()


def local(queries, routing, windows, shifts, library):
    n_z = lax.axis_size("range") // 2
    n_x = lax.axis_size("blk") // 4
    q_count, width = queries.shape
    lib_dev = library.shape[0]
    n_off = shifts.shape[0]
    cap = q_count // 4
    pair = 2 * cap
    n_pos = n_z // 2
    pieces = 2
    spectrum = width + LANES
    bf16, f32 = jnp.bfloat16, jnp.float32
    dma = pltpu.SemaphoreType.DMA
    vmem = pl.BlockSpec(memory_space=pltpu.VMEM)
    out = pl.pallas_call(
        functools.partial(kernel, n_z, n_x, (q_count, width, cap, n_off)),
        out_shape=jax.ShapeDtypeStruct((n_off, q_count), f32),
        in_specs=[vmem, vmem, vmem, pl.BlockSpec(memory_space=pltpu.SMEM), vmem],
        out_specs=vmem,
        scratch_shapes=[
            pltpu.VMEM((n_z, pair, spectrum), bf16),
            pltpu.VMEM((n_z, pair, spectrum), bf16),
            pltpu.VMEM((n_pos, 2, 4, pair, spectrum), bf16),
            pltpu.VMEM((n_pos, pair, spectrum), bf16),
            pltpu.VMEM((n_x, pieces, width // pieces, lib_dev), bf16),
            pltpu.VMEM((n_x, width + 2 * PAD, lib_dev), f32),
            pltpu.VMEM((n_x, width, n_off * lib_dev), bf16),
            pltpu.VMEM((2, 16 * pair, n_x * lib_dev), f32),
            pltpu.VMEM((2, n_off, 16 * pair, lib_dev), f32),
            pltpu.VMEM((n_pos, 2, 4, pair, LANES), f32),
            pltpu.VMEM((8, n_off, LANES), f32),
            pltpu.VMEM((8, n_off, LANES), f32),
            pltpu.VMEM((n_off, LANES), f32),
            pltpu.VMEM((n_z, n_off, LANES), f32),
            dma((n_z,)), dma((n_z,)),
            dma((3, n_pos)), dma((3, n_pos)),
            dma((4, n_pos)), dma((4, n_pos)),
            dma((n_x - 1, pieces)), dma((n_x - 1, pieces)),
            dma((8,)), dma((8,)),
            dma((n_z,)), dma((n_z,)),
        ],
        compiler_params=pltpu.CompilerParams(
            collective_id=0, has_side_effects=True, vmem_limit_bytes=56 * 1024 * 1024
        ),
    )(queries, routing.T, windows.T, shifts, library)
    return out.T


def solution(mesh):
    both = ("range", "blk")
    in_specs = (P(both, None), P(both, None), P(both, None), P(), P(both, None))
    return jax.shard_map(
        local, mesh=mesh, in_specs=in_specs, out_specs=P(both, None), check_vma=False
    )
```

```python
import functools

import jax
import jax.numpy as jnp
from jax import lax
from jax.experimental import pallas as pl
from jax.experimental.pallas import tpu as pltpu
from jax.sharding import PartitionSpec as P

MESH = pl.DeviceIdType.MESH
LANES = 128
PAD = 256
INVERSE = (0, 2, 1, 3)


def kernel(
    n_z, n_x, sizes,
    q_ref, routing_ref, windows_ref, shifts_ref, lib_ref, out_ref,
    tx, rx, groups, other, lt, padded, shifted, weight, acc, res, part_out, part, total, ret,
    z_send, z_recv, y_send, y_recv, sib_send, sib_recv, lib_send, lib_recv,
    part_send, part_recv, ret_send, ret_recv,
):
    q_count, width, cap, n_off = sizes
    n_pos = n_z // 2
    slots = 2 * n_z * cap
    pair = 2 * cap
    f32, bf16 = jnp.float32, jnp.bfloat16
    me = lax.axis_index("range")
    blk = lax.axis_index("blk")
    core = lax.rem(blk, 2)
    x = lax.rem(lax.div(blk, 2), n_x)
    yh = lax.div(blk, 2 * n_x)
    z = lax.div(me, 2)
    yl = lax.rem(me, 2)
    y = yh * 2 + yl

    def device(dz, dy, dx, dc):
        y_there = lax.rem(y + dy, 4)
        x_there = lax.rem(x + dx, n_x)
        return {
            "range": lax.rem(z + dz, n_z) * 2 + lax.rem(y_there, 2),
            "blk": lax.div(y_there, 2) * (2 * n_x) + x_there * 2 + lax.rem(core + dc, 2),
        }

    def remote(src, dst, send, recv, there):
        return pltpu.make_async_remote_copy(
            src_ref=src, dst_ref=dst, send_sem=send, recv_sem=recv,
            device_id=there, device_id_type=MESH,
        )

    y_step = (0, 1, 3, 2)
    barrier = pltpu.get_barrier_semaphore()
    greeted = [device(dz, 0, 0, 0) for dz in range(1, n_z)]
    greeted += [device(0, y_step[k], 0, dc) for k in range(4) for dc in range(2) if k or dc]
    greeted += [device(0, 0, dx, 0) for dx in (1, n_x - 1)]
    for there in greeted:
        pl.semaphore_signal(barrier, inc=1, device_id=there, device_id_type=MESH)

    t_row = routing_ref[...].astype(f32)
    p = lax.broadcasted_iota(jnp.int32, (q_count, q_count), 0)
    c = lax.broadcasted_iota(jnp.int32, (q_count, q_count), 1)
    t_column = jnp.sum(jnp.where(p == c, t_row, 0.0), axis=1, keepdims=True)
    earlier = (t_column == t_row) & (p < c)
    place = jnp.sum(jnp.where(earlier, 1.0, 0.0), axis=0, keepdims=True)
    slot_row = t_row * cap + place
    r = lax.broadcasted_iota(jnp.int32, (slots, q_count), 0).astype(f32)
    table = jnp.where(r == slot_row, 1.0, 0.0).astype(bf16)
    tx[:, :, :width] = (
        jnp.dot(table, q_ref[...], preferred_element_type=f32).astype(bf16).reshape(n_z, pair, width)
    )
    first = windows_ref[0:1, :]
    last = windows_ref[1:2, :]
    line = lax.broadcasted_iota(jnp.int32, (LANES, q_count), 0)
    coded = jnp.where(
        line == 0, lax.div(first, 64),
        jnp.where(line == 1, lax.rem(first, 64),
                  jnp.where(line == 2, lax.div(last, 64),
                            jnp.where(line == 3, lax.rem(last, 64), 0))))
    coded = coded.astype(f32).astype(bf16)
    tx[:, :, width:] = (
        lax.dot_general(table, coded, (((1,), (1,)), ((), ())), preferred_element_type=f32)
        .astype(bf16).reshape(n_z, pair, LANES)
    )
    rx[z] = tx[z]

    for b in range(n_x):
        padded[b, :PAD, :] = jnp.zeros((PAD, LANES), f32)
        padded[b, PAD + width:, :] = jnp.zeros((PAD, LANES), f32)
    for pos in range(n_pos):
        acc[pos] = jnp.zeros(acc.shape[1:], f32)

    pl.semaphore_wait(barrier, len(greeted))

    def z_copy(dz):
        there = lax.rem(z + dz, n_z)
        return remote(tx.at[there], rx.at[z], z_send.at[there], z_recv.at[z], device(dz, 0, 0, 0))

    def z_from(source):
        return remote(
            tx.at[source], rx.at[source], z_send.at[source], z_recv.at[source],
            device(lax.rem(source - z + n_z, n_z), 0, 0, 0),
        )

    def lib_copy(way, k):
        source, landing, dx = ((0, 2, 1), (0, 1, n_x - 1), (2, 3, 1), (1, 3, n_x - 1))[way]
        slot = min(way, 2)
        return remote(
            lt.at[source, k], lt.at[landing, k], lib_send.at[slot, k], lib_recv.at[slot, k],
            device(0, 0, dx, 0),
        )

    z_order = [1, n_z - 1, 2, n_z - 2, 3, n_z - 3, 4]
    for dz in z_order:
        z_copy(dz).start()
    pieces = lt.shape[1]
    depth = width // pieces
    split = pieces // 2
    for k in range(pieces):
        block = lib_ref[:, k * depth:(k + 1) * depth].astype(f32).T
        padded[0, PAD + k * depth:PAD + (k + 1) * depth, :] = block
        lt[0, k] = block.astype(bf16)
        if k % split == split - 1:
            for i in range(k - split + 1, k + 1):
                lib_copy(k // split, i).start()
    for i in range(split):
        lib_copy(0, split + i).start()
        lib_copy(1, i).start()

    def forward(i):
        lib_copy(0, i).wait_recv()
        lib_copy(2, i).start()
        lib_copy(1, split + i).wait_recv()
        lib_copy(3, split + i).start()

    def lib_ways(b):
        if b == 3:
            return [(2, i) for i in range(split)] + [(3, split + i) for i in range(split)]
        if b == 2:
            return [(0, split + i) for i in range(split)]
        return [(1, i) for i in range(split)]

    rows = 256

    def shift_block(b):
        def one(step, carry):
            o = lax.div(step, width // rows)
            at = pl.multiple_of(lax.rem(step, width // rows) * rows, rows)
            lane = pl.multiple_of(o * LANES, LANES)
            moved = padded[b, pl.ds(PAD + shifts_ref[o] + at, rows), :]
            shifted[b, pl.ds(at, rows), pl.ds(lane, LANES)] = moved.astype(bf16)
            return carry

        lax.fori_loop(0, n_off * (width // rows), one, 0)

    def take_block(b):
        for way, k in lib_ways(b):
            lib_copy(way, k).wait_recv()
        for k in range(pieces):
            padded[b, PAD + k * depth:PAD + (k + 1) * depth, :] = lt[b, k].astype(f32)
        shift_block(b)

    pr = lax.broadcasted_iota(jnp.int32, (2 * pair, 2 * pair), 0)
    pc = lax.broadcasted_iota(jnp.int32, (2 * pair, 2 * pair), 1)
    upper = lax.div(pr, pair)
    source_half = jnp.where(upper == 0, yl, 1 - yl)
    within = lax.rem(pr, pair)
    from_row = lax.div(within, cap) * pair + source_half * cap + lax.rem(within, cap)
    pick = jnp.where(pc == from_row, 1.0, 0.0).astype(bf16)
    home = lax.div(z, 2)
    odd = lax.rem(z, 2)
    hop = (0, n_pos - 1 - odd * (n_pos - 2), 1 + odd * (n_pos - 2), 2)

    def y_copy(k, pos):
        src = groups.at[pos, 0, 0] if k == 3 else other.at[pos]
        landing = INVERSE[k]
        return remote(
            src, groups.at[pos, 0, landing], y_send.at[k - 1, pos], y_recv.at[landing - 1, pos],
            device(0, y_step[k], 0, 0),
        )

    def y_from(k, pos):
        return remote(
            other.at[pos], groups.at[pos, 0, k], y_send.at[k - 1, pos], y_recv.at[k - 1, pos],
            device(0, y_step[k], 0, 0),
        )

    def sib_copy(k, pos):
        return remote(
            groups.at[pos, 0, k], groups.at[pos, 1, k], sib_send.at[k, pos], sib_recv.at[k, pos],
            device(0, 0, 0, 1),
        )

    def send_pos(pos):
        u = lax.rem(home + hop[pos], n_pos)
        for i in range(2):
            source = u * 2 + i

            @pl.when(source != z)
            def _():
                z_from(source).wait_recv()

        piece = rx[pl.ds(u * 2, 2)].reshape(2 * pair, width + LANES)
        parted = jnp.dot(pick, piece, preferred_element_type=f32).astype(bf16)
        groups[pos, 0, 0] = parted[:pair]
        other[pos] = parted[pair:]
        for k in (3, 1, 2):
            y_copy(k, pos).start()
        sib_copy(0, pos).start()

    def relay(pos):
        for k in (1, 2, 3):
            y_from(k, pos).wait_recv()
            sib_copy(k, pos).start()

    def settle(pos):
        for k in range(4):
            sib_copy(k, pos).wait_recv()

    wide = n_x * LANES
    col = lax.broadcasted_iota(jnp.int32, (1, wide), 1)
    nth = lax.div(col, LANES)
    away = jnp.where(nth == 2, n_x - 1, jnp.where(nth == 3, 2, nth))
    block_at = yh * (2 * n_x) + lax.rem(x + away, n_x) * 2 + core
    index = (block_at * LANES + lax.rem(col, LANES)).astype(f32)
    m = 8 * pair

    def weigh(pos):
        bounds = groups[pos, :, :, :, width:].reshape(m, LANES).astype(f32)
        lane = lax.broadcasted_iota(jnp.int32, (m, LANES), 1)
        low = jnp.sum(
            jnp.where(lane == 0, bounds * 64.0, jnp.where(lane == 1, bounds, 0.0)), axis=1, keepdims=True
        )
        high = jnp.sum(
            jnp.where(lane == 2, bounds * 64.0, jnp.where(lane == 3, bounds, 0.0)), axis=1, keepdims=True
        )
        inside = jnp.where((index >= low) & (index < high), 1.0, 0.0)
        for b in range(n_x):
            weight[pos, b] = inside[:, b * LANES:(b + 1) * LANES]

    def score(pos, count, *blocks):
        spectra = groups[pos:pos + count, :, :, :, :width].reshape(count * m, width)
        for b in blocks:
            for half in range(2):
                at = half * 4 * LANES
                scores = jnp.dot(spectra, shifted[b, :, at:at + 4 * LANES], preferred_element_type=f32)
                for i in range(4):
                    level = jnp.maximum(scores[:, i * LANES:(i + 1) * LANES], 0.0)
                    kept = (level * level).reshape(count, m, LANES) * weight[pos:pos + count, b]
                    acc[pos:pos + count, half * 4 + i] += kept

    def gather_scores(pos):
        lane = lax.broadcasted_iota(jnp.int32, (m, LANES), 1)
        value = jnp.zeros((m, LANES), f32)
        for o in range(n_off):
            value = jnp.where(lane == o, jnp.sum(acc[pos, o], axis=1, keepdims=True), value)
        res[pos] = value.reshape(2, 4, pair, LANES)

    shift_block(0)
    send_pos(0)
    forward(0)
    send_pos(1)
    forward(1)
    relay(0)
    send_pos(2)
    relay(1)
    send_pos(3)
    settle(0)
    settle(1)
    weigh(0)
    weigh(1)
    take_block(1)
    take_block(2)
    relay(2)
    score(0, 2, 0, 1)
    relay(3)
    settle(2)
    weigh(2)
    score(0, 3, 2)
    score(2, 1, 0, 1)
    take_block(3)
    settle(3)
    weigh(3)
    score(0, 4, 3)
    score(3, 1, 0, 1, 2)
    for pos in range(n_pos):
        gather_scores(pos)

    def part_copy(k, dc):
        return remote(
            part_out.at[2 * k + dc], part.at[2 * INVERSE[k] + dc],
            part_send.at[2 * k + dc], part_recv.at[2 * INVERSE[k] + dc],
            device(0, y_step[k], 0, dc),
        )

    def part_from(k, dc):
        return remote(
            part_out.at[2 * k + dc], part.at[2 * k + dc],
            part_send.at[2 * k + dc], part_recv.at[2 * k + dc],
            device(0, y_step[k], 0, dc),
        )

    lane = lax.broadcasted_iota(jnp.int32, (n_off, LANES), 1)
    mine = lax.div(lane, LANES // 2) == yl
    partners = [(k, dc) for k in (3, 1, 2, 0) for dc in range(2) if k or dc]
    for k, dc in partners + [(0, 0)]:
        column = res[:, dc, k].reshape(n_pos * pair, LANES)
        tile = jnp.concatenate([column, column], axis=0).T[:n_off]
        part_out[2 * k + dc] = jnp.where(mine, tile, 0.0)
        if k or dc:
            part_copy(k, dc).start()
    summed = part_out[0]
    for k, dc in partners:
        part_from(k, dc).wait_recv()
        summed = summed + part[2 * k + dc]
    total[...] = summed

    def ret_copy(dz):
        there = lax.rem(z + dz, n_z)
        return remote(total, ret.at[z], ret_send.at[there], ret_recv.at[z], device(dz, 0, 0, 0))

    def ret_from(dz):
        source = lax.rem(z + dz, n_z)
        return remote(
            total, ret.at[source], ret_send.at[source], ret_recv.at[source], device(dz, 0, 0, 0)
        )

    for dz in [4] + z_order[:-1][::-1]:
        ret_copy(dz).start()
    ret[z] = summed

    for dz in z_order:
        z_copy(dz).wait_send()
    for way, k in [(w, k) for w in range(2) for k in range(pieces)] + lib_ways(3):
        lib_copy(way, k).wait_send()
    for pos in range(n_pos):
        for k in (1, 2, 3):
            y_copy(k, pos).wait_send()
        for k in range(4):
            sib_copy(k, pos).wait_send()
    for k, dc in partners:
        part_copy(k, dc).wait_send()

    half_row = jnp.floor(t_row * 0.5)
    z_there = half_row
    yl_there = t_row - 2.0 * half_row
    delta = home.astype(f32) - jnp.floor(z_there * 0.5)
    delta = jnp.where(delta < 0.0, delta + n_pos, delta)
    z_odd = z_there - 2.0 * jnp.floor(z_there * 0.5)
    second = jnp.where(z_odd == 0.0, n_pos - 1.0, 1.0)
    pos_there = jnp.where(delta == 0.0, 0.0, jnp.where(delta == second, 1.0, jnp.where(delta == 2.0, 3.0, 2.0)))
    spot = (
        z_there * LANES + yl_there * (LANES // 2) + pos_there * pair
        + lax.rem(z, 2).astype(f32) * cap + place
    )
    line = lax.broadcasted_iota(jnp.int32, (n_z * LANES, q_count), 0).astype(f32)
    choose = jnp.where(line == spot, 1.0, 0.0)

    for dz in z_order:
        ret_from(dz).wait_recv()
    every = jnp.concatenate([ret[i] for i in range(n_z)], axis=1)
    answer = jnp.dot(every, choose, precision=lax.Precision.HIGHEST, preferred_element_type=f32)
    span = (last - first).astype(f32) * float(width)
    out_ref[...] = answer / span

    for dz in z_order:
        ret_copy(dz).wait_send()


def local(queries, routing, windows, shifts, library):
    n_z = lax.axis_size("range") // 2
    n_x = lax.axis_size("blk") // 4
    q_count, width = queries.shape
    lib_dev = library.shape[0]
    n_off = shifts.shape[0]
    cap = q_count // 4
    pair = 2 * cap
    n_pos = n_z // 2
    pieces = 4
    spectrum = width + LANES
    bf16, f32 = jnp.bfloat16, jnp.float32
    dma = pltpu.SemaphoreType.DMA
    vmem = pl.BlockSpec(memory_space=pltpu.VMEM)
    out = pl.pallas_call(
        functools.partial(kernel, n_z, n_x, (q_count, width, cap, n_off)),
        out_shape=jax.ShapeDtypeStruct((n_off, q_count), f32),
        in_specs=[vmem, vmem, vmem, pl.BlockSpec(memory_space=pltpu.SMEM), vmem],
        out_specs=vmem,
        scratch_shapes=[
            pltpu.VMEM((n_z, pair, spectrum), bf16),
            pltpu.VMEM((n_z, pair, spectrum), bf16),
            pltpu.VMEM((n_pos, 2, 4, pair, spectrum), bf16),
            pltpu.VMEM((n_pos, pair, spectrum), bf16),
            pltpu.VMEM((n_x, pieces, width // pieces, lib_dev), bf16),
            pltpu.VMEM((n_x, width + 2 * PAD, lib_dev), f32),
            pltpu.VMEM((n_x, width, n_off * lib_dev), bf16),
            pltpu.VMEM((n_pos, n_x, 8 * pair, lib_dev), f32),
            pltpu.VMEM((n_pos, n_off, 8 * pair, lib_dev), f32),
            pltpu.VMEM((n_pos, 2, 4, pair, LANES), f32),
            pltpu.VMEM((8, n_off, LANES), f32),
            pltpu.VMEM((8, n_off, LANES), f32),
            pltpu.VMEM((n_off, LANES), f32),
            pltpu.VMEM((n_z, n_off, LANES), f32),
            dma((n_z,)), dma((n_z,)),
            dma((3, n_pos)), dma((3, n_pos)),
            dma((4, n_pos)), dma((4, n_pos)),
            dma((3, pieces)), dma((3, pieces)),
            dma((8,)), dma((8,)),
            dma((n_z,)), dma((n_z,)),
        ],
        compiler_params=pltpu.CompilerParams(
            collective_id=0, has_side_effects=True, vmem_limit_bytes=56 * 1024 * 1024
        ),
    )(queries, routing.T, windows.T, shifts, library)
    return out.T


def solution(mesh):
    both = ("range", "blk")
    in_specs = (P(both, None), P(both, None), P(both, None), P(), P(both, None))
    return jax.shard_map(
        local, mesh=mesh, in_specs=in_specs, out_specs=P(both, None), check_vma=False
    )
```

```python
import functools

import jax
import jax.numpy as jnp
from jax import lax
from jax.experimental import pallas as pl
from jax.experimental.pallas import tpu as pltpu
from jax.sharding import PartitionSpec as P

MESH = pl.DeviceIdType.MESH
LANES = 128
PAD = 256
INVERSE = (0, 2, 1, 3)


def kernel(
    n_z, n_x, sizes,
    q_ref, routing_ref, windows_ref, shifts_ref, lib_ref, out_ref,
    tx, rx, groups, other, lt, padded, shifted, weight, acc, res, part_out, part, total, ret,
    z_send, z_recv, y_send, y_recv, sib_send, sib_recv, lib_send, lib_recv,
    part_send, part_recv, ret_send, ret_recv,
):
    q_count, width, cap, n_off = sizes
    n_pos = n_z // 2
    slots = 2 * n_z * cap
    pair = 2 * cap
    f32, bf16 = jnp.float32, jnp.bfloat16
    me = lax.axis_index("range")
    blk = lax.axis_index("blk")
    core = lax.rem(blk, 2)
    x = lax.rem(lax.div(blk, 2), n_x)
    yh = lax.div(blk, 2 * n_x)
    z = lax.div(me, 2)
    yl = lax.rem(me, 2)
    y = yh * 2 + yl

    def device(dz, dy, dx, dc):
        y_there = lax.rem(y + dy, 4)
        x_there = lax.rem(x + dx, n_x)
        return {
            "range": lax.rem(z + dz, n_z) * 2 + lax.rem(y_there, 2),
            "blk": lax.div(y_there, 2) * (2 * n_x) + x_there * 2 + lax.rem(core + dc, 2),
        }

    def remote(src, dst, send, recv, there):
        return pltpu.make_async_remote_copy(
            src_ref=src, dst_ref=dst, send_sem=send, recv_sem=recv,
            device_id=there, device_id_type=MESH,
        )

    y_step = (0, 1, 3, 2)
    barrier = pltpu.get_barrier_semaphore()
    greeted = [device(dz, 0, 0, 0) for dz in range(1, n_z)]
    greeted += [device(0, y_step[k], 0, dc) for k in range(4) for dc in range(2) if k or dc]
    greeted += [device(0, 0, dx, 0) for dx in (1, n_x - 1)]
    for there in greeted:
        pl.semaphore_signal(barrier, inc=1, device_id=there, device_id_type=MESH)

    t_row = routing_ref[...].astype(f32)
    p = lax.broadcasted_iota(jnp.int32, (q_count, q_count), 0)
    c = lax.broadcasted_iota(jnp.int32, (q_count, q_count), 1)
    t_column = jnp.sum(jnp.where(p == c, t_row, 0.0), axis=1, keepdims=True)
    earlier = (t_column == t_row) & (p < c)
    place = jnp.sum(jnp.where(earlier, 1.0, 0.0), axis=0, keepdims=True)
    slot_row = t_row * cap + place
    r = lax.broadcasted_iota(jnp.int32, (slots, q_count), 0).astype(f32)
    table = jnp.where(r == slot_row, 1.0, 0.0).astype(bf16)
    tx[:, :, :width] = (
        jnp.dot(table, q_ref[...], preferred_element_type=f32).astype(bf16).reshape(n_z, pair, width)
    )
    first = windows_ref[0:1, :]
    last = windows_ref[1:2, :]
    line = lax.broadcasted_iota(jnp.int32, (LANES, q_count), 0)
    coded = jnp.where(
        line == 0, lax.div(first, 64),
        jnp.where(line == 1, lax.rem(first, 64),
                  jnp.where(line == 2, lax.div(last, 64),
                            jnp.where(line == 3, lax.rem(last, 64), 0))))
    coded = coded.astype(f32).astype(bf16)
    tx[:, :, width:] = (
        lax.dot_general(table, coded, (((1,), (1,)), ((), ())), preferred_element_type=f32)
        .astype(bf16).reshape(n_z, pair, LANES)
    )
    rx[z] = tx[z]

    for b in range(n_x):
        padded[b, :PAD, :] = jnp.zeros((PAD, LANES), f32)
        padded[b, PAD + width:, :] = jnp.zeros((PAD, LANES), f32)
    for pos in range(n_pos):
        acc[pos] = jnp.zeros(acc.shape[1:], f32)

    pl.semaphore_wait(barrier, len(greeted))

    def z_copy(dz):
        there = lax.rem(z + dz, n_z)
        return remote(tx.at[there], rx.at[z], z_send.at[there], z_recv.at[z], device(dz, 0, 0, 0))

    def z_from(source):
        return remote(
            tx.at[source], rx.at[source], z_send.at[source], z_recv.at[source],
            device(lax.rem(source - z + n_z, n_z), 0, 0, 0),
        )

    def lib_copy(way, k):
        source, landing, dx = ((0, 2, 1), (0, 1, n_x - 1), (2, 3, 1), (1, 3, n_x - 1))[way]
        slot = min(way, 2)
        return remote(
            lt.at[source, k], lt.at[landing, k], lib_send.at[slot, k], lib_recv.at[slot, k],
            device(0, 0, dx, 0),
        )

    z_order = [1, n_z - 1, 2, n_z - 2, 3, n_z - 3, 4]
    for dz in z_order:
        z_copy(dz).start()
    pieces = lt.shape[1]
    depth = width // pieces
    split = pieces // 2
    for k in range(pieces):
        block = lib_ref[:, k * depth:(k + 1) * depth].astype(f32).T
        padded[0, PAD + k * depth:PAD + (k + 1) * depth, :] = block
        lt[0, k] = block.astype(bf16)
        if k % split == split - 1:
            for i in range(k - split + 1, k + 1):
                lib_copy(k // split, i).start()
    for i in range(split):
        lib_copy(0, split + i).start()
        lib_copy(1, i).start()

    def forward(i):
        lib_copy(0, i).wait_recv()
        lib_copy(2, i).start()
        lib_copy(1, split + i).wait_recv()
        lib_copy(3, split + i).start()

    def lib_ways(b):
        if b == 3:
            return [(2, i) for i in range(split)] + [(3, split + i) for i in range(split)]
        if b == 2:
            return [(0, split + i) for i in range(split)]
        return [(1, i) for i in range(split)]

    rows = 256

    def shift_block(b):
        def one(step, carry):
            o = lax.div(step, width // rows)
            at = pl.multiple_of(lax.rem(step, width // rows) * rows, rows)
            lane = pl.multiple_of(o * LANES, LANES)
            moved = padded[b, pl.ds(PAD + shifts_ref[o] + at, rows), :]
            shifted[b, pl.ds(at, rows), pl.ds(lane, LANES)] = moved.astype(bf16)
            return carry

        lax.fori_loop(0, n_off * (width // rows), one, 0)

    def take_block(b):
        for way, k in lib_ways(b):
            lib_copy(way, k).wait_recv()
        for k in range(pieces):
            padded[b, PAD + k * depth:PAD + (k + 1) * depth, :] = lt[b, k].astype(f32)
        shift_block(b)

    pr = lax.broadcasted_iota(jnp.int32, (2 * pair, 2 * pair), 0)
    pc = lax.broadcasted_iota(jnp.int32, (2 * pair, 2 * pair), 1)
    upper = lax.div(pr, pair)
    source_half = jnp.where(upper == 0, yl, 1 - yl)
    within = lax.rem(pr, pair)
    from_row = lax.div(within, cap) * pair + source_half * cap + lax.rem(within, cap)
    pick = jnp.where(pc == from_row, 1.0, 0.0).astype(bf16)
    home = lax.div(z, 2)
    odd = lax.rem(z, 2)
    hop = (0, n_pos - 1 - odd * (n_pos - 2), 1 + odd * (n_pos - 2), 2)

    def y_copy(k, pos):
        src = groups.at[pos, 0, 0] if k == 3 else other.at[pos]
        landing = INVERSE[k]
        return remote(
            src, groups.at[pos, 0, landing], y_send.at[k - 1, pos], y_recv.at[landing - 1, pos],
            device(0, y_step[k], 0, 0),
        )

    def y_from(k, pos):
        return remote(
            other.at[pos], groups.at[pos, 0, k], y_send.at[k - 1, pos], y_recv.at[k - 1, pos],
            device(0, y_step[k], 0, 0),
        )

    def sib_copy(k, pos):
        return remote(
            groups.at[pos, 0, k], groups.at[pos, 1, k], sib_send.at[k, pos], sib_recv.at[k, pos],
            device(0, 0, 0, 1),
        )

    def send_pos(pos):
        u = lax.rem(home + hop[pos], n_pos)
        for i in range(2):
            source = u * 2 + i

            @pl.when(source != z)
            def _():
                z_from(source).wait_recv()

        piece = rx[pl.ds(u * 2, 2)].reshape(2 * pair, width + LANES)
        parted = jnp.dot(pick, piece, preferred_element_type=f32).astype(bf16)
        groups[pos, 0, 0] = parted[:pair]
        other[pos] = parted[pair:]
        for k in (3, 1, 2):
            y_copy(k, pos).start()
        sib_copy(0, pos).start()

    def relay(pos):
        for k in (1, 2, 3):
            y_from(k, pos).wait_recv()
            sib_copy(k, pos).start()

    def settle(pos):
        for k in range(4):
            sib_copy(k, pos).wait_recv()

    wide = n_x * LANES
    col = lax.broadcasted_iota(jnp.int32, (1, wide), 1)
    nth = lax.div(col, LANES)
    away = jnp.where(nth == 2, n_x - 1, jnp.where(nth == 3, 2, nth))
    block_at = yh * (2 * n_x) + lax.rem(x + away, n_x) * 2 + core
    index = (block_at * LANES + lax.rem(col, LANES)).astype(f32)
    m = 8 * pair

    def weigh(pos):
        bounds = groups[pos, :, :, :, width:].reshape(m, LANES).astype(f32)
        lane = lax.broadcasted_iota(jnp.int32, (m, LANES), 1)
        low = jnp.sum(
            jnp.where(lane == 0, bounds * 64.0, jnp.where(lane == 1, bounds, 0.0)), axis=1, keepdims=True
        )
        high = jnp.sum(
            jnp.where(lane == 2, bounds * 64.0, jnp.where(lane == 3, bounds, 0.0)), axis=1, keepdims=True
        )
        inside = jnp.where((index >= low) & (index < high), 1.0, 0.0)
        for b in range(n_x):
            weight[pos, b] = inside[:, b * LANES:(b + 1) * LANES]

    def score(pos, count, *blocks):
        spectra = groups[pos:pos + count, :, :, :, :width].reshape(count * m, width)
        for b in blocks:
            for half in range(2):
                at = half * 4 * LANES
                scores = jnp.dot(spectra, shifted[b, :, at:at + 4 * LANES], preferred_element_type=f32)
                for i in range(4):
                    level = jnp.maximum(scores[:, i * LANES:(i + 1) * LANES], 0.0)
                    kept = (level * level).reshape(count, m, LANES) * weight[pos:pos + count, b]
                    acc[pos:pos + count, half * 4 + i] += kept

    def gather_scores(pos):
        lane = lax.broadcasted_iota(jnp.int32, (m, LANES), 1)
        value = jnp.zeros((m, LANES), f32)
        for o in range(n_off):
            value = jnp.where(lane == o, jnp.sum(acc[pos, o], axis=1, keepdims=True), value)
        res[pos] = value.reshape(2, 4, pair, LANES)

    shift_block(0)
    send_pos(0)
    forward(0)
    send_pos(1)
    forward(1)
    send_pos(2)
    relay(0)
    take_block(1)
    relay(1)
    settle(0)
    weigh(0)
    score(0, 1, 0)
    send_pos(3)
    settle(1)
    weigh(1)
    score(0, 1, 1)
    score(1, 1, 0, 1)
    relay(2)
    take_block(2)
    score(0, 2, 2)
    settle(2)
    weigh(2)
    score(2, 1, 0)
    relay(3)
    score(2, 1, 1, 2)
    take_block(3)
    settle(3)
    weigh(3)
    score(0, 4, 3)
    score(3, 1, 0, 1, 2)
    for pos in range(n_pos):
        gather_scores(pos)

    def part_copy(k, dc):
        return remote(
            part_out.at[2 * k + dc], part.at[2 * INVERSE[k] + dc],
            part_send.at[2 * k + dc], part_recv.at[2 * INVERSE[k] + dc],
            device(0, y_step[k], 0, dc),
        )

    def part_from(k, dc):
        return remote(
            part_out.at[2 * k + dc], part.at[2 * k + dc],
            part_send.at[2 * k + dc], part_recv.at[2 * k + dc],
            device(0, y_step[k], 0, dc),
        )

    lane = lax.broadcasted_iota(jnp.int32, (n_off, LANES), 1)
    mine = lax.div(lane, LANES // 2) == yl
    partners = [(k, dc) for k in (3, 1, 2, 0) for dc in range(2) if k or dc]
    for k, dc in partners + [(0, 0)]:
        column = res[:, dc, k].reshape(n_pos * pair, LANES)
        tile = jnp.concatenate([column, column], axis=0).T[:n_off]
        part_out[2 * k + dc] = jnp.where(mine, tile, 0.0)
        if k or dc:
            part_copy(k, dc).start()
    summed = part_out[0]
    for k, dc in partners:
        part_from(k, dc).wait_recv()
        summed = summed + part[2 * k + dc]
    total[...] = summed

    def ret_copy(dz):
        there = lax.rem(z + dz, n_z)
        return remote(total, ret.at[z], ret_send.at[there], ret_recv.at[z], device(dz, 0, 0, 0))

    def ret_from(dz):
        source = lax.rem(z + dz, n_z)
        return remote(
            total, ret.at[source], ret_send.at[source], ret_recv.at[source], device(dz, 0, 0, 0)
        )

    for dz in [4] + z_order[:-1][::-1]:
        ret_copy(dz).start()
    ret[z] = summed

    for dz in z_order:
        z_copy(dz).wait_send()
    for way, k in [(w, k) for w in range(2) for k in range(pieces)] + lib_ways(3):
        lib_copy(way, k).wait_send()
    for pos in range(n_pos):
        for k in (1, 2, 3):
            y_copy(k, pos).wait_send()
        for k in range(4):
            sib_copy(k, pos).wait_send()
    for k, dc in partners:
        part_copy(k, dc).wait_send()

    half_row = jnp.floor(t_row * 0.5)
    z_there = half_row
    yl_there = t_row - 2.0 * half_row
    delta = home.astype(f32) - jnp.floor(z_there * 0.5)
    delta = jnp.where(delta < 0.0, delta + n_pos, delta)
    z_odd = z_there - 2.0 * jnp.floor(z_there * 0.5)
    second = jnp.where(z_odd == 0.0, n_pos - 1.0, 1.0)
    pos_there = jnp.where(delta == 0.0, 0.0, jnp.where(delta == second, 1.0, jnp.where(delta == 2.0, 3.0, 2.0)))
    spot = (
        z_there * LANES + yl_there * (LANES // 2) + pos_there * pair
        + lax.rem(z, 2).astype(f32) * cap + place
    )
    line = lax.broadcasted_iota(jnp.int32, (n_z * LANES, q_count), 0).astype(f32)
    choose = jnp.where(line == spot, 1.0, 0.0)

    for dz in z_order:
        ret_from(dz).wait_recv()
    every = jnp.concatenate([ret[i] for i in range(n_z)], axis=1)
    answer = jnp.dot(every, choose, precision=lax.Precision.HIGHEST, preferred_element_type=f32)
    span = (last - first).astype(f32) * float(width)
    out_ref[...] = answer / span

    for dz in z_order:
        ret_copy(dz).wait_send()


def local(queries, routing, windows, shifts, library):
    n_z = lax.axis_size("range") // 2
    n_x = lax.axis_size("blk") // 4
    q_count, width = queries.shape
    lib_dev = library.shape[0]
    n_off = shifts.shape[0]
    cap = q_count // 4
    pair = 2 * cap
    n_pos = n_z // 2
    pieces = 4
    spectrum = width + LANES
    bf16, f32 = jnp.bfloat16, jnp.float32
    dma = pltpu.SemaphoreType.DMA
    vmem = pl.BlockSpec(memory_space=pltpu.VMEM)
    out = pl.pallas_call(
        functools.partial(kernel, n_z, n_x, (q_count, width, cap, n_off)),
        out_shape=jax.ShapeDtypeStruct((n_off, q_count), f32),
        in_specs=[vmem, vmem, vmem, pl.BlockSpec(memory_space=pltpu.SMEM), vmem],
        out_specs=vmem,
        scratch_shapes=[
            pltpu.VMEM((n_z, pair, spectrum), bf16),
            pltpu.VMEM((n_z, pair, spectrum), bf16),
            pltpu.VMEM((n_pos, 2, 4, pair, spectrum), bf16),
            pltpu.VMEM((n_pos, pair, spectrum), bf16),
            pltpu.VMEM((n_x, pieces, width // pieces, lib_dev), bf16),
            pltpu.VMEM((n_x, width + 2 * PAD, lib_dev), f32),
            pltpu.VMEM((n_x, width, n_off * lib_dev), bf16),
            pltpu.VMEM((n_pos, n_x, 8 * pair, lib_dev), f32),
            pltpu.VMEM((n_pos, n_off, 8 * pair, lib_dev), f32),
            pltpu.VMEM((n_pos, 2, 4, pair, LANES), f32),
            pltpu.VMEM((8, n_off, LANES), f32),
            pltpu.VMEM((8, n_off, LANES), f32),
            pltpu.VMEM((n_off, LANES), f32),
            pltpu.VMEM((n_z, n_off, LANES), f32),
            dma((n_z,)), dma((n_z,)),
            dma((3, n_pos)), dma((3, n_pos)),
            dma((4, n_pos)), dma((4, n_pos)),
            dma((3, pieces)), dma((3, pieces)),
            dma((8,)), dma((8,)),
            dma((n_z,)), dma((n_z,)),
        ],
        compiler_params=pltpu.CompilerParams(
            collective_id=0, has_side_effects=True, vmem_limit_bytes=56 * 1024 * 1024
        ),
    )(queries, routing.T, windows.T, shifts, library)
    return out.T


def solution(mesh):
    both = ("range", "blk")
    in_specs = (P(both, None), P(both, None), P(both, None), P(), P(both, None))
    return jax.shard_map(
        local, mesh=mesh, in_specs=in_specs, out_specs=P(both, None), check_vma=False
    )
```

```python
import functools

import jax
import jax.numpy as jnp
from jax import lax
from jax.experimental import pallas as pl
from jax.experimental.pallas import tpu as pltpu
from jax.sharding import PartitionSpec as P

MESH = pl.DeviceIdType.MESH
LANES = 128
PAD = 256
INVERSE = (0, 2, 1, 3)


def kernel(
    n_z, n_x, sizes,
    q_ref, routing_ref, windows_ref, shifts_ref, lib_ref, out_ref,
    tx, rx, groups, other, lt, padded, shifted, weight, acc, res, part_out, part, total, ret,
    z_send, z_recv, y_send, y_recv, sib_send, sib_recv, lib_send, lib_recv,
    part_send, part_recv, ret_send, ret_recv,
):
    q_count, width, cap, n_off = sizes
    n_pos = n_z // 2
    slots = 2 * n_z * cap
    pair = 2 * cap
    f32, bf16 = jnp.float32, jnp.bfloat16
    me = lax.axis_index("range")
    blk = lax.axis_index("blk")
    core = lax.rem(blk, 2)
    x = lax.rem(lax.div(blk, 2), n_x)
    yh = lax.div(blk, 2 * n_x)
    z = lax.div(me, 2)
    yl = lax.rem(me, 2)
    y = yh * 2 + yl

    def device(dz, dy, dx, dc):
        y_there = lax.rem(y + dy, 4)
        x_there = lax.rem(x + dx, n_x)
        return {
            "range": lax.rem(z + dz, n_z) * 2 + lax.rem(y_there, 2),
            "blk": lax.div(y_there, 2) * (2 * n_x) + x_there * 2 + lax.rem(core + dc, 2),
        }

    def remote(src, dst, send, recv, there):
        return pltpu.make_async_remote_copy(
            src_ref=src, dst_ref=dst, send_sem=send, recv_sem=recv,
            device_id=there, device_id_type=MESH,
        )

    y_step = (0, 1, 3, 2)
    barrier = pltpu.get_barrier_semaphore()
    greeted = [device(dz, 0, 0, 0) for dz in range(1, n_z)]
    greeted += [device(0, y_step[k], 0, dc) for k in range(4) for dc in range(2) if k or dc]
    greeted += [device(0, 0, dx, 0) for dx in (1, n_x - 1)]
    for there in greeted:
        pl.semaphore_signal(barrier, inc=1, device_id=there, device_id_type=MESH)

    t_row = routing_ref[...].astype(f32)
    p = lax.broadcasted_iota(jnp.int32, (q_count, q_count), 0)
    c = lax.broadcasted_iota(jnp.int32, (q_count, q_count), 1)
    t_column = jnp.sum(jnp.where(p == c, t_row, 0.0), axis=1, keepdims=True)
    earlier = (t_column == t_row) & (p < c)
    place = jnp.sum(jnp.where(earlier, 1.0, 0.0), axis=0, keepdims=True)
    slot_row = t_row * cap + place
    r = lax.broadcasted_iota(jnp.int32, (slots, q_count), 0).astype(f32)
    table = jnp.where(r == slot_row, 1.0, 0.0).astype(bf16)
    tx[:, :, :width] = (
        jnp.dot(table, q_ref[...], preferred_element_type=f32).astype(bf16).reshape(n_z, pair, width)
    )
    first = windows_ref[0:1, :]
    last = windows_ref[1:2, :]
    line = lax.broadcasted_iota(jnp.int32, (LANES, q_count), 0)
    coded = jnp.where(
        line == 0, lax.div(first, 64),
        jnp.where(line == 1, lax.rem(first, 64),
                  jnp.where(line == 2, lax.div(last, 64),
                            jnp.where(line == 3, lax.rem(last, 64), 0))))
    coded = coded.astype(f32).astype(bf16)
    tx[:, :, width:] = (
        lax.dot_general(table, coded, (((1,), (1,)), ((), ())), preferred_element_type=f32)
        .astype(bf16).reshape(n_z, pair, LANES)
    )
    rx[z] = tx[z]

    for b in range(n_x):
        padded[b, :PAD, :] = jnp.zeros((PAD, LANES), f32)
        padded[b, PAD + width:, :] = jnp.zeros((PAD, LANES), f32)
    for pos in range(n_pos):
        acc[pos] = jnp.zeros(acc.shape[1:], f32)

    pl.semaphore_wait(barrier, len(greeted))

    def z_copy(dz):
        there = lax.rem(z + dz, n_z)
        return remote(tx.at[there], rx.at[z], z_send.at[there], z_recv.at[z], device(dz, 0, 0, 0))

    def z_from(source):
        return remote(
            tx.at[source], rx.at[source], z_send.at[source], z_recv.at[source],
            device(lax.rem(source - z + n_z, n_z), 0, 0, 0),
        )

    def lib_copy(way, k):
        source, landing, dx = ((0, 2, 1), (0, 1, n_x - 1), (2, 3, 1), (1, 3, n_x - 1))[way]
        slot = min(way, 2)
        return remote(
            lt.at[source, k], lt.at[landing, k], lib_send.at[slot, k], lib_recv.at[slot, k],
            device(0, 0, dx, 0),
        )

    z_order = [1, n_z - 1, 2, n_z - 2, 3, n_z - 3, 4]
    turn = 1 - 2 * lax.rem(z, 2)
    for d in (1, -1, 2, -2, 3, -3, 4):
        z_copy(lax.rem(n_z + d * turn, n_z)).start()
    pieces = lt.shape[1]
    depth = width // pieces
    split = pieces // 2
    for k in range(pieces):
        block = lib_ref[:, k * depth:(k + 1) * depth].astype(f32).T
        padded[0, PAD + k * depth:PAD + (k + 1) * depth, :] = block
        lt[0, k] = block.astype(bf16)
        if k % split == split - 1:
            for i in range(k - split + 1, k + 1):
                lib_copy(k // split, i).start()
    for i in range(split):
        lib_copy(0, split + i).start()
        lib_copy(1, i).start()

    def forward(i):
        lib_copy(0, i).wait_recv()
        lib_copy(2, i).start()
        lib_copy(1, split + i).wait_recv()
        lib_copy(3, split + i).start()

    def lib_ways(b):
        if b == 3:
            return [(2, i) for i in range(split)] + [(3, split + i) for i in range(split)]
        if b == 2:
            return [(0, split + i) for i in range(split)]
        return [(1, i) for i in range(split)]

    rows = 256

    def shift_block(b):
        def one(step, carry):
            o = lax.div(step, width // rows)
            at = pl.multiple_of(lax.rem(step, width // rows) * rows, rows)
            lane = pl.multiple_of(o * LANES, LANES)
            moved = padded[b, pl.ds(PAD + shifts_ref[o] + at, rows), :]
            shifted[b, pl.ds(at, rows), pl.ds(lane, LANES)] = moved.astype(bf16)
            return carry

        lax.fori_loop(0, n_off * (width // rows), one, 0)

    def take_block(b):
        for way, k in lib_ways(b):
            lib_copy(way, k).wait_recv()
        for k in range(pieces):
            padded[b, PAD + k * depth:PAD + (k + 1) * depth, :] = lt[b, k].astype(f32)
        shift_block(b)

    pr = lax.broadcasted_iota(jnp.int32, (2 * pair, 2 * pair), 0)
    pc = lax.broadcasted_iota(jnp.int32, (2 * pair, 2 * pair), 1)
    upper = lax.div(pr, pair)
    source_half = jnp.where(upper == 0, yl, 1 - yl)
    within = lax.rem(pr, pair)
    from_row = lax.div(within, cap) * pair + source_half * cap + lax.rem(within, cap)
    pick = jnp.where(pc == from_row, 1.0, 0.0).astype(bf16)
    home = lax.div(z, 2)
    odd = lax.rem(z, 2)
    hop = (0, n_pos - 1 - odd * (n_pos - 2), 1 + odd * (n_pos - 2), 2)

    def y_copy(k, pos):
        src = groups.at[pos, 0, 0] if k == 3 else other.at[pos]
        landing = INVERSE[k]
        return remote(
            src, groups.at[pos, 0, landing], y_send.at[k - 1, pos], y_recv.at[landing - 1, pos],
            device(0, y_step[k], 0, 0),
        )

    def y_from(k, pos):
        return remote(
            other.at[pos], groups.at[pos, 0, k], y_send.at[k - 1, pos], y_recv.at[k - 1, pos],
            device(0, y_step[k], 0, 0),
        )

    def sib_copy(k, pos):
        return remote(
            groups.at[pos, 0, k], groups.at[pos, 1, k], sib_send.at[k, pos], sib_recv.at[k, pos],
            device(0, 0, 0, 1),
        )

    def send_pos(pos):
        u = lax.rem(home + hop[pos], n_pos)
        for i in range(2):
            source = u * 2 + i

            @pl.when(source != z)
            def _():
                z_from(source).wait_recv()

        piece = rx[pl.ds(u * 2, 2)].reshape(2 * pair, width + LANES)
        parted = jnp.dot(pick, piece, preferred_element_type=f32).astype(bf16)
        groups[pos, 0, 0] = parted[:pair]
        other[pos] = parted[pair:]
        for k in (3, 1, 2):
            y_copy(k, pos).start()
        sib_copy(0, pos).start()

    def relay(pos):
        for k in (1, 2, 3):
            y_from(k, pos).wait_recv()
            sib_copy(k, pos).start()

    def settle(pos):
        for k in range(4):
            sib_copy(k, pos).wait_recv()

    wide = n_x * LANES
    col = lax.broadcasted_iota(jnp.int32, (1, wide), 1)
    nth = lax.div(col, LANES)
    away = jnp.where(nth == 2, n_x - 1, jnp.where(nth == 3, 2, nth))
    block_at = yh * (2 * n_x) + lax.rem(x + away, n_x) * 2 + core
    index = (block_at * LANES + lax.rem(col, LANES)).astype(f32)
    m = 8 * pair

    def weigh(pos):
        bounds = groups[pos, :, :, :, width:].reshape(m, LANES).astype(f32)
        lane = lax.broadcasted_iota(jnp.int32, (m, LANES), 1)
        low = jnp.sum(
            jnp.where(lane == 0, bounds * 64.0, jnp.where(lane == 1, bounds, 0.0)), axis=1, keepdims=True
        )
        high = jnp.sum(
            jnp.where(lane == 2, bounds * 64.0, jnp.where(lane == 3, bounds, 0.0)), axis=1, keepdims=True
        )
        inside = jnp.where((index >= low) & (index < high), 1.0, 0.0)
        for b in range(n_x):
            weight[pos, b] = inside[:, b * LANES:(b + 1) * LANES]

    def score(pos, count, *blocks):
        spectra = groups[pos:pos + count, :, :, :, :width].reshape(count * m, width)
        for b in blocks:
            for half in range(2):
                at = half * 4 * LANES
                scores = jnp.dot(spectra, shifted[b, :, at:at + 4 * LANES], preferred_element_type=f32)
                for i in range(4):
                    level = jnp.maximum(scores[:, i * LANES:(i + 1) * LANES], 0.0)
                    kept = (level * level).reshape(count, m, LANES) * weight[pos:pos + count, b]
                    acc[pos:pos + count, half * 4 + i] += kept

    def gather_scores(pos):
        lane = lax.broadcasted_iota(jnp.int32, (m, LANES), 1)
        value = jnp.zeros((m, LANES), f32)
        for o in range(n_off):
            value = jnp.where(lane == o, jnp.sum(acc[pos, o], axis=1, keepdims=True), value)
        res[pos] = value.reshape(2, 4, pair, LANES)

    shift_block(0)
    send_pos(0)
    forward(0)
    send_pos(1)
    forward(1)
    send_pos(2)
    relay(0)
    take_block(1)
    relay(1)
    settle(0)
    weigh(0)
    score(0, 1, 0)
    send_pos(3)
    settle(1)
    weigh(1)
    score(0, 1, 1)
    score(1, 1, 0, 1)
    relay(2)
    take_block(2)
    score(0, 2, 2)
    settle(2)
    weigh(2)
    score(2, 1, 0, 1, 2)
    take_block(3)
    relay(3)
    score(0, 3, 3)
    for pos in range(n_pos - 1):
        gather_scores(pos)
    settle(3)
    weigh(3)
    score(3, 1, 0, 1, 2, 3)
    gather_scores(n_pos - 1)

    def part_copy(k, dc):
        return remote(
            part_out.at[2 * k + dc], part.at[2 * INVERSE[k] + dc],
            part_send.at[2 * k + dc], part_recv.at[2 * INVERSE[k] + dc],
            device(0, y_step[k], 0, dc),
        )

    def part_from(k, dc):
        return remote(
            part_out.at[2 * k + dc], part.at[2 * k + dc],
            part_send.at[2 * k + dc], part_recv.at[2 * k + dc],
            device(0, y_step[k], 0, dc),
        )

    lane = lax.broadcasted_iota(jnp.int32, (n_off, LANES), 1)
    mine = lax.div(lane, LANES // 2) == yl
    partners = [(k, dc) for k in (3, 1, 2, 0) for dc in range(2) if k or dc]
    for k, dc in partners + [(0, 0)]:
        column = res[:, dc, k].reshape(n_pos * pair, LANES)
        tile = jnp.concatenate([column, column], axis=0).T[:n_off]
        part_out[2 * k + dc] = jnp.where(mine, tile, 0.0)
        if k or dc:
            part_copy(k, dc).start()
    summed = part_out[0]
    for k, dc in partners:
        part_from(k, dc).wait_recv()
        summed = summed + part[2 * k + dc]
    total[...] = summed

    def ret_copy(dz):
        there = lax.rem(z + dz, n_z)
        return remote(total, ret.at[z], ret_send.at[there], ret_recv.at[z], device(dz, 0, 0, 0))

    def ret_from(dz):
        source = lax.rem(z + dz, n_z)
        return remote(
            total, ret.at[source], ret_send.at[source], ret_recv.at[source], device(dz, 0, 0, 0)
        )

    for dz in [4] + z_order[:-1][::-1]:
        ret_copy(dz).start()
    ret[z] = summed

    for dz in z_order:
        z_copy(dz).wait_send()
    for way, k in [(w, k) for w in range(2) for k in range(pieces)] + lib_ways(3):
        lib_copy(way, k).wait_send()
    for pos in range(n_pos):
        for k in (1, 2, 3):
            y_copy(k, pos).wait_send()
        for k in range(4):
            sib_copy(k, pos).wait_send()
    for k, dc in partners:
        part_copy(k, dc).wait_send()

    half_row = jnp.floor(t_row * 0.5)
    z_there = half_row
    yl_there = t_row - 2.0 * half_row
    delta = home.astype(f32) - jnp.floor(z_there * 0.5)
    delta = jnp.where(delta < 0.0, delta + n_pos, delta)
    z_odd = z_there - 2.0 * jnp.floor(z_there * 0.5)
    second = jnp.where(z_odd == 0.0, n_pos - 1.0, 1.0)
    pos_there = jnp.where(delta == 0.0, 0.0, jnp.where(delta == second, 1.0, jnp.where(delta == 2.0, 3.0, 2.0)))
    spot = (
        z_there * LANES + yl_there * (LANES // 2) + pos_there * pair
        + lax.rem(z, 2).astype(f32) * cap + place
    )
    line = lax.broadcasted_iota(jnp.int32, (n_z * LANES, q_count), 0).astype(f32)
    choose = jnp.where(line == spot, 1.0, 0.0).astype(bf16)

    for dz in z_order:
        ret_from(dz).wait_recv()
    every = jnp.concatenate([ret[i] for i in range(n_z)], axis=1)
    high = every.astype(bf16).astype(f32)
    middle = (every - high).astype(bf16).astype(f32)
    thirds = jnp.concatenate([high, middle, every - high - middle], axis=0).astype(bf16)
    picked = jnp.dot(thirds, choose, preferred_element_type=f32)
    answer = picked[2 * n_off:] + picked[n_off:2 * n_off] + picked[:n_off]
    span = (last - first).astype(f32) * float(width)
    out_ref[...] = answer / span

    for dz in z_order:
        ret_copy(dz).wait_send()


def local(queries, routing, windows, shifts, library):
    n_z = lax.axis_size("range") // 2
    n_x = lax.axis_size("blk") // 4
    q_count, width = queries.shape
    lib_dev = library.shape[0]
    n_off = shifts.shape[0]
    cap = q_count // 4
    pair = 2 * cap
    n_pos = n_z // 2
    pieces = 4
    spectrum = width + LANES
    bf16, f32 = jnp.bfloat16, jnp.float32
    dma = pltpu.SemaphoreType.DMA
    vmem = pl.BlockSpec(memory_space=pltpu.VMEM)
    out = pl.pallas_call(
        functools.partial(kernel, n_z, n_x, (q_count, width, cap, n_off)),
        out_shape=jax.ShapeDtypeStruct((n_off, q_count), f32),
        in_specs=[vmem, vmem, vmem, pl.BlockSpec(memory_space=pltpu.SMEM), vmem],
        out_specs=vmem,
        scratch_shapes=[
            pltpu.VMEM((n_z, pair, spectrum), bf16),
            pltpu.VMEM((n_z, pair, spectrum), bf16),
            pltpu.VMEM((n_pos, 2, 4, pair, spectrum), bf16),
            pltpu.VMEM((n_pos, pair, spectrum), bf16),
            pltpu.VMEM((n_x, pieces, width // pieces, lib_dev), bf16),
            pltpu.VMEM((n_x, width + 2 * PAD, lib_dev), f32),
            pltpu.VMEM((n_x, width, n_off * lib_dev), bf16),
            pltpu.VMEM((n_pos, n_x, 8 * pair, lib_dev), f32),
            pltpu.VMEM((n_pos, n_off, 8 * pair, lib_dev), f32),
            pltpu.VMEM((n_pos, 2, 4, pair, LANES), f32),
            pltpu.VMEM((8, n_off, LANES), f32),
            pltpu.VMEM((8, n_off, LANES), f32),
            pltpu.VMEM((n_off, LANES), f32),
            pltpu.VMEM((n_z, n_off, LANES), f32),
            dma((n_z,)), dma((n_z,)),
            dma((3, n_pos)), dma((3, n_pos)),
            dma((4, n_pos)), dma((4, n_pos)),
            dma((3, pieces)), dma((3, pieces)),
            dma((8,)), dma((8,)),
            dma((n_z,)), dma((n_z,)),
        ],
        compiler_params=pltpu.CompilerParams(
            collective_id=0, has_side_effects=True, vmem_limit_bytes=56 * 1024 * 1024
        ),
    )(queries, routing.T, windows.T, shifts, library)
    return out.T


def solution(mesh):
    both = ("range", "blk")
    in_specs = (P(both, None), P(both, None), P(both, None), P(), P(both, None))
    return jax.shard_map(
        local, mesh=mesh, in_specs=in_specs, out_specs=P(both, None), check_vma=False
    )
```
